256 devices in a mesh: gx: 16 (over z_lo, x), gy: 4 (over z_hi, core), gz: 4 (over y).
Axes of the slice: x: 4, y: 4, z: 8 (z_hi: 2, z_lo: 4; z = z_hi * 4 + z_lo), core: 2. Of those that a mesh axis runs over, the one named last changes fastest.
Arguments:
- order_parameter: float32 [64, 512, 512], P('gx', 'gy', 'gz'), may hold values from -1 to 1
- dissolved_species: float32 [64, 512, 512], P('gx', 'gy', 'gz'), may hold values from -0.8 to 0.2
- broad_undercool: float32 [128, 128, 16], P('gy', 'gz'), may hold values from -2.4 to 2.4
Outputs:
- phase_out: float32 [64, 512, 512], P('gx', 'gy', 'gz')
- solute_out: float32 [64, 512, 512], P('gx', 'gy', 'gz')
- temperature_out: float32 [128, 128, 16], P('gy', 'gz')
The draws below stay inside these ranges and needn't reach their ends.
All inputs are finite; a program needn't handle non-finite values.
Results may differ from the reference program's by a relative error of at most 0.0001.
Values sent between devices are 32-bit elements; how exact they have to be, the bound alone decides.
A program may use at most 64 MiB of HBM per device.

```python
import jax
import jax.numpy as jnp

FACTOR = 4
SUBSTEPS = 4
NX = 64
NY = 512
NZ = 512
BROAD_COUNT_ONE = 16
BROAD_COUNT_TWO = 128
BROAD_COUNT_THREE = 128


def shard_levels(key, dims, pieces, smallest, largest):
    level, own = 1.0, jax.random.fold_in(key, 6)
    for axis_at, parts in pieces:
        steps = jnp.exp(jax.random.uniform(jax.random.fold_in(own, axis_at), (parts,), jnp.float32, smallest / len(pieces), largest / len(pieces)))
        level = level * jnp.repeat(steps, dims[axis_at] // parts).reshape([-1 if axis == axis_at else 1 for axis in range(len(dims))])
    return level


def noise(stream_key, extent, width, bound, cuts=(), dtype=jnp.bfloat16):
    entries = width * jax.random.normal(stream_key, extent, jnp.float32)
    if cuts:
        entries = entries * shard_levels(stream_key, extent, cuts, -0.22, 0.18)
    return jnp.clip(entries, -bound, bound).astype(dtype)


def setup_inputs(seed: int = 0) -> dict:
    keys = jax.random.split(jax.random.key(seed), 4)
    order_parameter = jnp.clip(jax.random.uniform(keys[0], (NX, NY, NZ), jnp.float32, -1.0, 1.0) * shard_levels(keys[0], (NX, NY, NZ), ((0, 16), (1, 4), (2, 4)), -0.4, 0.0), -1.0, 1.0)
    dissolved_species = jnp.clip(-0.8 + 1 * jax.random.uniform(keys[1], (NX, NY, NZ), jnp.float32) ** shard_levels(keys[1], (NX, NY, NZ), ((0, 16), (1, 4), (2, 4)), -0.2, 0.2), -0.8, 0.2)
    broad_undercool = noise(keys[2], (BROAD_COUNT_TWO, BROAD_COUNT_THREE, BROAD_COUNT_ONE), 0.4, 2.4, ((0, 4), (1, 4)), jnp.float32)
    return {"order_parameter": order_parameter, "dissolved_species": dissolved_species, "broad_undercool": broad_undercool}


TIME_INCREMENT = 0.1
COUPLING = 3.0
PARTITION = 0.3
DIFFUSION = 1.0
THERMAL_SPREAD = 1.2
FREEZING_WARMTH = 2.0


def second_derivative_sum(field):
    total = -6.0 * field
    for axis_id in range(3):
        total = total + jnp.roll(field, 1, axis_id) + jnp.roll(field, -1, axis_id)
    return total


def faces_flux(values, mobility):
    total = jnp.zeros_like(values)
    for axis_id in range(3):
        upper_v = jnp.roll(values, -1, axis_id)
        lower_v = jnp.roll(values, 1, axis_id)
        upper_m = jnp.roll(mobility, -1, axis_id)
        lower_m = jnp.roll(mobility, 1, axis_id)
        total = total + 0.5 * (upper_m + mobility) * (upper_v - values) - 0.5 * (mobility + lower_m) * (values - lower_v)
    return total


def reference(order_parameter, dissolved_species, broad_undercool):
    for substep in range(SUBSTEPS):
        vertical_pile = jnp.transpose(broad_undercool, (2, 0, 1))
        fine_temp = jnp.repeat(jnp.repeat(jnp.repeat(vertical_pile, FACTOR, 0), FACTOR, 1), FACTOR, 2)
        square = 1.0 - order_parameter * order_parameter
        driving = second_derivative_sum(order_parameter) + order_parameter - order_parameter * order_parameter * order_parameter - COUPLING * square * square * (dissolved_species + fine_temp)
        new_phase = jnp.clip(order_parameter + TIME_INCREMENT * driving, -1.0, 1.0)
        change = new_phase - order_parameter
        mobility = 0.5 * (1.0 - new_phase)
        numer = TIME_INCREMENT * DIFFUSION * faces_flux(dissolved_species, mobility) + 0.5 * (1.0 + (1.0 - PARTITION) * dissolved_species) * change
        new_solute = dissolved_species + numer / (0.5 * (1.0 + PARTITION - (1.0 - PARTITION) * new_phase))
        blocks = (0.5 * change).reshape(BROAD_COUNT_ONE, FACTOR, BROAD_COUNT_TWO, FACTOR, BROAD_COUNT_THREE, FACTOR)
        freezing_warmth_source = jnp.transpose(jnp.mean(blocks, axis=(1, 3, 5)), (1, 2, 0))
        broad_undercool = broad_undercool + TIME_INCREMENT * THERMAL_SPREAD * second_derivative_sum(broad_undercool) + FREEZING_WARMTH * freezing_warmth_source
        order_parameter = new_phase
        dissolved_species = new_solute
    return order_parameter, dissolved_species, broad_undercool
```

```python
import jax
import jax.numpy as jnp
from jax import lax
from jax.experimental import pallas as pl
from jax.experimental.pallas import tpu as pltpu
from jax.sharding import PartitionSpec as P

MESH = pl.DeviceIdType.MESH
HIGH = lax.Precision.HIGHEST
SUBSTEPS = 4
NGX, NGY, NGZ = 16, 4, 4
SX, SY, SZ = 4, 128, 128
CY = 32
PAD = 8
ROWS = 32


def lanes(shape):
    return lax.broadcasted_iota(jnp.int32, shape, len(shape) - 1)


def pack_plane(t):
    lane = lanes((8, 128))
    out = t[0:8]
    for k in range(1, 4):
        moved = pltpu.roll(t[8 * k : 8 * k + 8], 32 * k, 1)
        out = jnp.where(lane // 32 == k, moved, out)
    return out


def unpack_plane(tile):
    parts = [tile] + [pltpu.roll(tile, 128 - 32 * k, 1) for k in range(1, 4)]
    return jnp.concatenate(parts, axis=0)


def dot(a, b):
    return lax.dot_general(
        a, b, (((1,), (0,)), ((), ())), precision=HIGH, preferred_element_type=jnp.float32
    )


def kernel(
    phase_in, solute_in, temp_in,
    phase_out, solute_out, temp_out,
    ph, so, tcol, tp, fine,
    ysend, yrecv, zsend, zrecv,
    tsend, trecv, gath,
    load_sem,
    xp_s, xp_r, y_s, y_r, z_s, z_r, xu_s, xu_r, t_s, t_r, g_s, g_r,
):
    gx, gy, gz = lax.axis_index("gx"), lax.axis_index("gy"), lax.axis_index("gz")
    xdev = [{"gx": lax.rem(gx + NGX - 1, NGX)}, {"gx": lax.rem(gx + 1, NGX)}]
    ydev = [{"gy": lax.rem(gy + NGY - 1, NGY)}, {"gy": lax.rem(gy + 1, NGY)}]
    zdev = [{"gz": lax.rem(gz + NGZ - 1, NGZ)}, {"gz": lax.rem(gz + 1, NGZ)}]

    own = pl.ds(PAD, SY)
    loads = [
        pltpu.make_async_copy(phase_in, ph.at[0, pl.ds(1, SX), own], load_sem.at[0]),
        pltpu.make_async_copy(solute_in, so.at[0, pl.ds(1, SX), own], load_sem.at[1]),
        pltpu.make_async_copy(temp_in, tcol, load_sem.at[2]),
    ]
    for c in loads:
        c.start()

    barrier = pltpu.get_barrier_semaphore()
    for k in range(1, NGX):
        pl.semaphore_signal(
            barrier, inc=1, device_id={"gx": lax.rem(gx + k, NGX)}, device_id_type=MESH
        )
    for d in ydev + zdev:
        pl.semaphore_signal(barrier, inc=1, device_id=d, device_id_type=MESH)

    def remote(src, dst, s, r, dev):
        return pltpu.make_async_remote_copy(
            src_ref=src, dst_ref=dst, send_sem=s, recv_sem=r, device_id=dev, device_id_type=MESH
        )

    def xp_copy(slot, side):
        return remote(
            ph.at[slot, 1 if side == 0 else SX, own],
            ph.at[slot, SX + 1 if side == 0 else 0, own],
            xp_s.at[slot, side], xp_r.at[slot, side], xdev[side],
        )

    def xu_copy(slot, side):
        return remote(
            so.at[slot, 1 if side == 0 else SX, own],
            so.at[slot, SX + 1 if side == 0 else 0, own],
            xu_s.at[slot, side], xu_r.at[slot, side], xdev[side],
        )

    def y_copy(slot, side):
        return remote(
            ysend.at[slot, side], yrecv.at[slot, side], y_s.at[slot, side], y_r.at[slot, side], ydev[side]
        )

    def z_copy(slot, side):
        return remote(
            zsend.at[slot], zrecv.at[slot, side], z_s.at[slot, side], z_r.at[slot, side], zdev[side]
        )

    tdev = xdev + ydev + zdev

    def t_copy(slot, k):
        return remote(tsend.at[slot], trecv.at[slot, k], t_s.at[slot, k], t_r.at[slot, k], tdev[k])

    def g_copy(k):
        return remote(
            tsend.at[0], gath.at[gx], g_s.at[k], g_r.at[k], {"gx": lax.rem(gx + k, NGX)}
        )

    lane_z = lanes((SY, 128))

    def pack_y(pslot, uslot, slot):
        for side, row in ((0, PAD), (1, PAD + SY - 1)):
            for x in range(SX):
                ysend[slot, side, x : x + 1, :] = ph[pslot, x + 1, row : row + 1, :]
                ysend[slot, side, 4 + x : 5 + x, :] = so[uslot, x + 1, row : row + 1, :]

    def pack_z(pslot, uslot, slot):
        for c in range(SY // ROWS):
            lane = lanes((ROWS, 128))
            acc = jnp.zeros((ROWS, 128), jnp.float32)
            for x in range(SX):
                for f, (ref, sl) in enumerate(((ph, pslot), (so, uslot))):
                    v = ref[sl, x + 1, PAD + ROWS * c : PAD + ROWS * (c + 1), :]
                    l0 = x + 4 * f
                    acc = jnp.where(lane == l0, pltpu.roll(v, l0, 1) if l0 else v, acc)
                    acc = jnp.where(lane == l0 + 8, pltpu.roll(v, l0 + 9, 1), acc)
            zsend[slot, ROWS * c : ROWS * (c + 1), :] = acc

    def unpack_y(pslot, uslot, slot):
        for x in range(SX):
            ph[pslot, x + 1, PAD + SY : PAD + SY + 1, :] = yrecv[slot, 0, x : x + 1, :]
            ph[pslot, x + 1, PAD - 1 : PAD, :] = yrecv[slot, 1, x : x + 1, :]

    def unpack_yu(uslot, slot):
        for x in range(SX):
            so[uslot, x + 1, PAD + SY : PAD + SY + 1, :] = yrecv[slot, 0, 4 + x : 5 + x, :]
            so[uslot, x + 1, PAD - 1 : PAD, :] = yrecv[slot, 1, 4 + x : 5 + x, :]

    def z_neighbours(v, slot, rows, l0):
        lane = lanes(v.shape)
        upper = zrecv[slot, 0, rows, :]
        lower = zrecv[slot, 1, rows, :]
        vm = jnp.where(lane == 0, pltpu.roll(lower, 128 - (l0 + 8), 1), pltpu.roll(v, 1, 1))
        vp = jnp.where(lane == 127, pltpu.roll(upper, 127 - l0, 1), pltpu.roll(v, 127, 1))
        return vm, vp

    def phase_layer(x, old, new, uslot, slot):
        for c in range(SY // ROWS):
            r = PAD + ROWS * c
            rows = pl.ds(ROWS * c, ROWS)
            p = ph[old, x + 1, r : r + ROWS, :]
            zm, zp = z_neighbours(p, slot, rows, x)
            total = (
                (ph[old, x, r : r + ROWS, :] + ph[old, x + 2, r : r + ROWS, :])
                + (ph[old, x + 1, r - 1 : r + ROWS - 1, :] + ph[old, x + 1, r + 1 : r + ROWS + 1, :])
                + (zm + zp)
            )
            square = 1.0 - p * p
            drive = so[uslot, x + 1, r : r + ROWS, :] + fine[rows, :]
            driving = (total - 6.0 * p) + p * square - 3.0 * (square * square) * drive
            ph[new, x + 1, r : r + ROWS, :] = jnp.clip(p + 0.1 * driving, -1.0, 1.0)

    def solute_layer(x, old, new, slot):
        for c in range(SY // ROWS):
            r = PAD + ROWS * c
            rows = pl.ds(ROWS * c, ROWS)
            p = ph[new, x + 1, r : r + ROWS, :]
            u = so[old, x + 1, r : r + ROWS, :]
            q = 2.0 - p
            pzm, pzp = z_neighbours(p, slot, rows, x)
            uzm, uzp = z_neighbours(u, slot, rows, x + 4)
            flux = (q - pzm) * (uzm - u) + (q - pzp) * (uzp - u)
            for dx, dr in ((0, 0), (2, 0), (1, -1), (1, 1)):
                pn = ph[new, x + dx, r + dr : r + dr + ROWS, :]
                un = so[old, x + dx, r + dr : r + dr + ROWS, :]
                flux = flux + (q - pn) * (un - u)
            change = p - ph[old, x + 1, r : r + ROWS, :]
            numer = 0.05 * flux + (1.0 + 0.7 * u) * change
            so[new, x + 1, r : r + ROWS, :] = u + numer / (1.3 - 0.7 * p)

    zi = lax.broadcasted_iota(jnp.int32, (128, 128), 0)
    zj = lax.broadcasted_iota(jnp.int32, (128, 128), 1)
    spread_z = jnp.where(zj // 4 == zi, 1.0, 0.0).astype(jnp.float32)
    pool_z = jnp.where(zi // 4 == zj, 1.0, 0.0).astype(jnp.float32)
    yi = lax.broadcasted_iota(jnp.int32, (128, CY), 0)
    yj = lax.broadcasted_iota(jnp.int32, (128, CY), 1)
    spread_y = jnp.where(yi // 4 == yj, 1.0, 0.0).astype(jnp.float32)
    wi = lax.broadcasted_iota(jnp.int32, (CY, 128), 0)
    wj = lax.broadcasted_iota(jnp.int32, (CY, 128), 1)
    pool_y = jnp.where(wj // 4 == wi, 1.0, 0.0).astype(jnp.float32)

    def set_fine():
        fine[...] = dot(spread_y, dot(tp[...], spread_z))

    for c in loads:
        c.wait()
    pl.semaphore_wait(barrier, NGX - 1 + 4)
    for side in range(2):
        xp_copy(0, side).start()
    pack_y(0, 0, 0)
    for side in range(2):
        y_copy(0, side).start()
    pack_z(0, 0, 0)
    for side in range(2):
        z_copy(0, side).start()
    for side in range(2):
        xu_copy(0, side).start()
    tp[...] = jnp.zeros((CY, 128), jnp.float32)
    tp[:, 0:32] = tcol[:, pl.ds(gx, 1), :].reshape(CY, 32)
    tsend[0] = pack_plane(tp[...])
    for k in range(6):
        t_copy(0, k).start()
    set_fine()

    def wait_phase(slot):
        for side in range(2):
            xp_copy(slot, side).wait()
            y_copy(slot, side).wait()
            z_copy(slot, side).wait()

    wait_phase(0)
    unpack_y(0, 0, 0)

    lane_t = lanes((CY, 128))
    row_t = lax.broadcasted_iota(jnp.int32, (CY, 128), 0)

    def substep(s, carry):
        old = lax.rem(s, 2)
        new = 1 - old
        for x, side in ((0, 0), (3, 1)):
            phase_layer(x, old, new, old, old)
            xp_copy(new, side).start()
        for x in (1, 2):
            phase_layer(x, old, new, old, old)
        pack_y(new, old, new)
        for side in range(2):
            y_copy(new, side).start()
        pack_z(new, old, new)
        for side in range(2):
            z_copy(new, side).start()
        change = ph[new, 1, PAD : PAD + SY, :] - ph[old, 1, PAD : PAD + SY, :]
        for x in range(1, SX):
            change = change + (ph[new, x + 1, PAD : PAD + SY, :] - ph[old, x + 1, PAD : PAD + SY, :])
        heat = dot(pool_y, dot(change, pool_z))
        for k in range(6):
            t_copy(old, k).wait()
        t = tp[...]
        planes = [unpack_plane(trecv[old, k]) for k in range(6)]
        ym = jnp.where(row_t == 0, pltpu.roll(planes[3], 1, 0), pltpu.roll(t, 1, 0))
        yp = jnp.where(row_t == CY - 1, pltpu.roll(planes[2], CY - 1, 0), pltpu.roll(t, CY - 1, 0))
        zm = jnp.where(lane_t == 0, pltpu.roll(planes[5], 128 - 31, 1), pltpu.roll(t, 1, 1))
        zp = jnp.where(lane_t == 31, pltpu.roll(planes[4], 31, 1), pltpu.roll(t, 127, 1))
        total = (planes[0] + planes[1]) + (ym + yp) + (zm + zp) - 6.0 * t
        t = t + 0.12 * total + (2.0 * 0.5 / 64.0) * heat
        t = jnp.where(lane_t < 32, t, 0.0)
        tp[...] = t
        tsend[new] = pack_plane(t)

        @pl.when(s < SUBSTEPS - 1)
        def _():
            for k in range(6):
                t_copy(new, k).start()

        @pl.when(s == SUBSTEPS - 1)
        def _():
            for k in range(1, NGX):
                g_copy(k).start()

        set_fine()
        wait_phase(new)
        for side in range(2):
            xu_copy(old, side).wait()
        unpack_y(new, old, new)
        unpack_yu(old, new)
        for x, side in ((0, 0), (3, 1)):
            solute_layer(x, old, new, new)

            @pl.when(s < SUBSTEPS - 1)
            def _():
                xu_copy(new, side).start()

        for x in (1, 2):
            solute_layer(x, old, new, new)
        return carry

    lax.fori_loop(0, SUBSTEPS, substep, 0)

    outs = [
        pltpu.make_async_copy(ph.at[0, pl.ds(1, SX), own], phase_out, load_sem.at[0]),
        pltpu.make_async_copy(so.at[0, pl.ds(1, SX), own], solute_out, load_sem.at[1]),
    ]
    for c in outs:
        c.start()
    for k in range(1, NGX):
        g_copy(k).wait()
    gath[gx] = tsend[0]
    for x in range(NGX):
        temp_out[x] = unpack_plane(gath[x])[:, 0:32]
    for c in outs:
        c.wait()


def per_device(order_parameter, dissolved_species, broad_undercool):
    temp = jnp.transpose(broad_undercool, (0, 2, 1))
    f32 = jnp.float32
    dma = pltpu.SemaphoreType.DMA
    phase, solute, temp = pl.pallas_call(
        kernel,
        out_shape=(
            jax.ShapeDtypeStruct((SX, SY, SZ), f32),
            jax.ShapeDtypeStruct((SX, SY, SZ), f32),
            jax.ShapeDtypeStruct((NGX, CY, 32), f32),
        ),
        in_specs=[pl.BlockSpec(memory_space=pl.ANY)] * 3,
        out_specs=(
            pl.BlockSpec(memory_space=pl.ANY),
            pl.BlockSpec(memory_space=pl.ANY),
            pl.BlockSpec(memory_space=pltpu.VMEM),
        ),
        scratch_shapes=[
            pltpu.VMEM((2, SX + 2, SY + 2 * PAD, SZ), f32),
            pltpu.VMEM((2, SX + 2, SY + 2 * PAD, SZ), f32),
            pltpu.VMEM((CY, NGX, 32), f32),
            pltpu.VMEM((CY, 128), f32),
            pltpu.VMEM((SY, SZ), f32),
            pltpu.VMEM((2, 2, 8, 128), f32),
            pltpu.VMEM((2, 2, 8, 128), f32),
            pltpu.VMEM((2, SY, 128), f32),
            pltpu.VMEM((2, 2, SY, 128), f32),
            pltpu.VMEM((2, 8, 128), f32),
            pltpu.VMEM((2, 6, 8, 128), f32),
            pltpu.VMEM((NGX, 8, 128), f32),
            dma((3,)),
            dma((2, 2)), dma((2, 2)),
            dma((2, 2)), dma((2, 2)),
            dma((2, 2)), dma((2, 2)),
            dma((2, 2)), dma((2, 2)),
            dma((2, 6)), dma((2, 6)),
            dma((NGX,)), dma((NGX,)),
        ],
        compiler_params=pltpu.CompilerParams(
            collective_id=0, has_side_effects=True, vmem_limit_bytes=32 * 1024 * 1024
        ),
        name="solidify",
    )(order_parameter, dissolved_species, temp)
    return phase, solute, jnp.transpose(temp, (1, 2, 0))


def solution(mesh):
    specs = (P("gx", "gy", "gz"), P("gx", "gy", "gz"), P("gy", "gz", None))
    return jax.shard_map(
        per_device, mesh=mesh, in_specs=specs, out_specs=specs, check_vma=False
    )
```

```python
import jax
import jax.numpy as jnp
from jax import lax
from jax.experimental import pallas as pl
from jax.experimental.pallas import tpu as pltpu
from jax.sharding import PartitionSpec as P

MESH = pl.DeviceIdType.MESH
HIGH = lax.Precision.HIGHEST
NGX, NGY, NGZ = 16, 4, 4
SX, SY, SZ = 4, 128, 128
CY = 32
PAD = 8
ROWS = 32
ORDER = (0, 3, 1, 2)
CHUNKS = SY // ROWS
PHASE, SOLUTE = 0, 1


def lanes(shape):
    return lax.broadcasted_iota(jnp.int32, shape, len(shape) - 1)


def roll(v, amount, axis=1):
    amount = amount % v.shape[axis]
    return pltpu.roll(v, amount, axis) if amount else v


def pack_plane(t):
    lane = lanes((8, 128))
    out = t[0:8]
    for k in range(1, 4):
        out = jnp.where(lane // 32 == k, roll(t[8 * k : 8 * k + 8], 32 * k), out)
    return out


def unpack_plane(tile):
    return jnp.concatenate([roll(tile, -32 * k) for k in range(4)], axis=0)


def dot(a, b):
    return lax.dot_general(
        a, b, (((1,), (0,)), ((), ())), precision=HIGH, preferred_element_type=jnp.float32
    )


def kernel(
    phase_in, solute_in, temp_in,
    phase_out, solute_out, temp_out,
    w, tcol, tp, fine,
    ysend, yrecv, zsend, zrecv, zhalo,
    tsend, trecv, gath,
    load_sem,
    x_s, x_r, y_s, y_r, z_s, z_r, t_s, t_r, g_s, g_r,
):
    gx, gy, gz = lax.axis_index("gx"), lax.axis_index("gy"), lax.axis_index("gz")
    xdev = [{"gx": lax.rem(gx + NGX - 1, NGX)}, {"gx": lax.rem(gx + 1, NGX)}]
    ydev = [{"gy": lax.rem(gy + NGY - 1, NGY)}, {"gy": lax.rem(gy + 1, NGY)}]
    zdev = [{"gz": lax.rem(gz + NGZ - 1, NGZ)}, {"gz": lax.rem(gz + 1, NGZ)}]
    tdev = xdev + ydev + zdev

    barrier = pltpu.get_barrier_semaphore()
    for k in range(1, NGX):
        pl.semaphore_signal(
            barrier, inc=1, device_id={"gx": lax.rem(gx + k, NGX)}, device_id_type=MESH
        )
    for d in ydev + zdev:
        pl.semaphore_signal(barrier, inc=1, device_id=d, device_id_type=MESH)

    own = pl.ds(PAD, SY)
    loads = [
        pltpu.make_async_copy(phase_in, w.at[0, pl.ds(1, SX), PHASE, own], load_sem.at[0]),
        pltpu.make_async_copy(solute_in, w.at[1, pl.ds(1, SX), SOLUTE, own], load_sem.at[1]),
        pltpu.make_async_copy(temp_in, tcol, load_sem.at[2]),
    ]
    for c in loads:
        c.start()

    def remote(src, dst, s, r, dev):
        return pltpu.make_async_remote_copy(
            src_ref=src, dst_ref=dst, send_sem=s, recv_sem=r, device_id=dev, device_id_type=MESH
        )

    def x_copy(slot, side, c, fields=pl.ds(0, 2)):
        rows = pl.ds(PAD + ROWS * c, ROWS)
        return remote(
            w.at[slot, 1 if side == 0 else SX, fields, rows],
            w.at[slot, SX + 1 if side == 0 else 0, fields, rows],
            x_s.at[slot, side, c], x_r.at[slot, side, c], xdev[side],
        )

    def y_copy(slot, side):
        return remote(
            ysend.at[slot, side], yrecv.at[slot, side], y_s.at[slot, side], y_r.at[slot, side], ydev[side]
        )

    def z_copy(slot, side):
        return remote(
            zsend.at[slot], zrecv.at[slot, side], z_s.at[slot, side], z_r.at[slot, side], zdev[side]
        )

    def t_copy(slot, k):
        return remote(tsend.at[slot], trecv.at[slot, k], t_s.at[slot, k], t_r.at[slot, k], tdev[k])

    def g_copy(k):
        return remote(
            tsend.at[0], gath.at[gx], g_s.at[k], g_r.at[k], {"gx": lax.rem(gx + k, NGX)}
        )

    def send_y(slot, fields=(PHASE, SOLUTE)):
        for side, row in ((0, PAD), (1, PAD + SY - 1)):
            for f in fields:
                for x in range(SX):
                    ysend[slot, side, 4 * f + x : 4 * f + x + 1, :] = w[slot, x + 1, f, row : row + 1, :]
            y_copy(slot, side).start()

    def send_z(slot, fields=(PHASE, SOLUTE)):
        lane = lanes((16, 128))
        acc = jnp.zeros((16, 128), jnp.float32)
        for g in range(8):
            for f in fields:
                for x in range(SX):
                    l0 = 16 * g + 2 * (x + 4 * f)
                    v = w[slot, x + 1, f, PAD + 16 * g : PAD + 16 * g + 16, :]
                    acc = jnp.where(lane // 2 == l0 // 2, roll(v, l0 + 1), acc)
        zsend[slot] = acc
        for side in range(2):
            z_copy(slot, side).start()

    def take_yz(slot, fields=(PHASE, SOLUTE)):
        for side in range(2):
            z_copy(slot, side).wait()
        lane = lanes((16, 128))
        zhalo[...] = jnp.where(
            lane % 2 == 0, roll(zrecv[slot, 0], -1), roll(zrecv[slot, 1], 1)
        )
        for side in range(2):
            y_copy(slot, side).wait()
        for f in fields:
            for x in range(SX):
                w[slot, x + 1, f, PAD + SY : PAD + SY + 1, :] = yrecv[slot, 0, 4 * f + x : 4 * f + x + 1, :]
                w[slot, x + 1, f, PAD - 1 : PAD, :] = yrecv[slot, 1, 4 * f + x : 4 * f + x + 1, :]

    def neighbours(slot, x, f, c):
        r = PAD + ROWS * c
        v = w[slot, x + 1, f, r : r + ROWS, :]
        lane = lanes((ROWS, 128))
        halo = jnp.concatenate(
            [roll(zhalo[...], 127 - (16 * g + 2 * (x + 4 * f))) for g in (2 * c, 2 * c + 1)], axis=0
        )
        return v, (
            w[slot, x, f, r : r + ROWS, :],
            w[slot, x + 2, f, r : r + ROWS, :],
            w[slot, x + 1, f, r - 1 : r + ROWS - 1, :],
            w[slot, x + 1, f, r + 1 : r + ROWS + 1, :],
            jnp.where(lane == 0, halo, roll(v, 1)),
            jnp.where(lane == 127, halo, roll(v, -1)),
        )

    def next_phase(p, near, u, c):
        total = (near[0] + near[1]) + (near[2] + near[3]) + (near[4] + near[5])
        square = 1.0 - p * p
        drive = u + fine[ROWS * c : ROWS * (c + 1), :]
        driving = (total - 6.0 * p) + p * square - 3.0 * (square * square) * drive
        return jnp.clip(p + 0.1 * driving, -1.0, 1.0)

    def next_solute(p, near, u, unear, before):
        q = 2.0 - p
        flux = (q - near[0]) * (unear[0] - u)
        for pn, un in zip(near[1:], unear[1:]):
            flux = flux + (q - pn) * (un - u)
        numer = 0.05 * flux + (1.0 + 0.7 * u) * (p - before)
        return u + numer / (1.3 - 0.7 * p)

    def first_phase(x, c):
        rows = pl.ds(PAD + ROWS * c, ROWS)
        p, near = neighbours(0, x, PHASE, c)
        w[1, x + 1, PHASE, rows, :] = next_phase(p, near, w[1, x + 1, SOLUTE, rows, :], c)

    def fused(x, c, a, b):
        rows = pl.ds(PAD + ROWS * c, ROWS)
        p, near = neighbours(a, x, PHASE, c)
        u, unear = neighbours(a, x, SOLUTE, c)
        u = next_solute(p, near, u, unear, w[b, x + 1, PHASE, rows, :])
        w[b, x + 1, SOLUTE, rows, :] = u
        w[b, x + 1, PHASE, rows, :] = next_phase(p, near, u, c)

    def last_solute(x, c):
        rows = pl.ds(PAD + ROWS * c, ROWS)
        p, near = neighbours(0, x, PHASE, c)
        u, unear = neighbours(0, x, SOLUTE, c)
        out = pl.ds(ROWS * c, ROWS)
        solute_out[x, out, :] = next_solute(p, near, u, unear, w[1, x + 1, PHASE, rows, :])
        phase_out[x, out, :] = p

    zi = lax.broadcasted_iota(jnp.int32, (128, 128), 0)
    zj = lax.broadcasted_iota(jnp.int32, (128, 128), 1)
    spread_z = jnp.where(zj // 4 == zi, 1.0, 0.0).astype(jnp.float32)
    pool_z = jnp.where(zi // 4 == zj, 1.0, 0.0).astype(jnp.float32)
    yi = lax.broadcasted_iota(jnp.int32, (128, CY), 0)
    yj = lax.broadcasted_iota(jnp.int32, (128, CY), 1)
    spread_y = jnp.where(yi // 4 == yj, 1.0, 0.0).astype(jnp.float32)
    wi = lax.broadcasted_iota(jnp.int32, (CY, 128), 0)
    wj = lax.broadcasted_iota(jnp.int32, (CY, 128), 1)
    pool_y = jnp.where(wj // 4 == wi, 1.0, 0.0).astype(jnp.float32)
    lane_t, row_t = wj, wi

    def set_fine():
        fine[...] = dot(spread_y, dot(tp[...], spread_z))

    def next_temp(a, b):
        change = w[b, 1, PHASE, own, :] - w[a, 1, PHASE, own, :]
        for x in range(1, SX):
            change = change + (w[b, x + 1, PHASE, own, :] - w[a, x + 1, PHASE, own, :])
        heat = dot(pool_y, dot(change, pool_z))
        for k in range(6):
            t_copy(a, k).wait()
        t = tp[...]
        planes = [unpack_plane(trecv[a, k]) for k in range(6)]
        ym = jnp.where(row_t == 0, roll(planes[3], 1, 0), roll(t, 1, 0))
        yp = jnp.where(row_t == CY - 1, roll(planes[2], -1, 0), roll(t, -1, 0))
        zm = jnp.where(lane_t == 0, roll(planes[5], -31), roll(t, 1))
        zp = jnp.where(lane_t == 31, roll(planes[4], 31), roll(t, -1))
        total = (planes[0] + planes[1]) + (ym + yp) + (zm + zp) - 6.0 * t
        t = t + 0.12 * total + (2.0 * 0.5 / 64.0) * heat
        t = jnp.where(lane_t < 32, t, 0.0)
        tp[...] = t
        tsend[b] = pack_plane(t)

    def layers(step, slot_in, slot_out, send, fields):
        for c in ORDER:
            for x in (1, 2):
                step(x, c)
        for c in ORDER:
            for x, side in ((0, 0), (3, 1)):
                x_copy(slot_in, 1 - side, c, fields).wait_recv()
                step(x, c)
                if send:
                    x_copy(slot_out, side, c).start()
            if send and c == ORDER[1]:
                send_y(slot_out)
        if send:
            send_z(slot_out)
        for c in ORDER:
            for side in range(2):
                x_copy(slot_in, side, c, fields).wait_send()

    only_phase = pl.ds(PHASE, 1)
    loads[0].wait()
    pl.semaphore_wait(barrier, NGX - 1 + 4)
    for c in ORDER:
        for side in range(2):
            x_copy(0, side, c, only_phase).start()
    ysend[...] = jnp.zeros_like(ysend)
    send_y(0, (PHASE,))
    send_z(0, (PHASE,))
    loads[2].wait()
    tp[...] = jnp.zeros((CY, 128), jnp.float32)
    tp[:, 0:32] = tcol[:, pl.ds(gx, 1), :].reshape(CY, 32)
    tsend[0] = pack_plane(tp[...])
    for k in range(6):
        t_copy(0, k).start()
    set_fine()
    loads[1].wait()
    take_yz(0, (PHASE,))
    layers(first_phase, 0, 1, True, only_phase)
    next_temp(0, 1)
    for k in range(6):
        t_copy(1, k).start()
    set_fine()

    def substep(r, carry):
        b = lax.rem(r, 2)
        a = 1 - b
        take_yz(a)
        layers(lambda x, c: fused(x, c, a, b), a, b, True, pl.ds(0, 2))
        next_temp(a, b)

        @pl.when(r < 4)
        def _():
            for k in range(6):
                t_copy(b, k).start()

        @pl.when(r == 4)
        def _():
            for k in range(1, NGX):
                g_copy(k).start()

        set_fine()
        return carry

    lax.fori_loop(2, 5, substep, 0)

    take_yz(0)
    layers(last_solute, 0, None, False, pl.ds(0, 2))
    for k in range(1, NGX):
        g_copy(k).wait()
    gath[gx] = tsend[0]
    for x in range(NGX):
        temp_out[:, x, :] = unpack_plane(gath[x])[:, 0:32]


def finish(phase, solute, temp, phase_out, solute_out, temp_out, sem):
    copies = [
        pltpu.make_async_copy(phase, phase_out, sem.at[0]),
        pltpu.make_async_copy(solute, solute_out, sem.at[1]),
        pltpu.make_async_copy(temp, temp_out, sem.at[2]),
    ]
    for c in copies:
        c.start()
    for c in copies:
        c.wait()


def per_device(order_parameter, dissolved_species, broad_undercool):
    temp = jnp.transpose(broad_undercool, (0, 2, 1))
    f32 = jnp.float32
    dma = pltpu.SemaphoreType.DMA
    vmem = pl.BlockSpec(memory_space=pltpu.VMEM)
    hbm = pl.BlockSpec(memory_space=pltpu.HBM)
    block = jax.ShapeDtypeStruct((SX, SY, SZ), f32)
    phase, solute, temp = pl.pallas_call(
        kernel,
        out_shape=(block, block, jax.ShapeDtypeStruct((CY, NGX, 32), f32)),
        in_specs=[hbm] * 3,
        out_specs=(vmem, vmem, vmem),
        scratch_shapes=[
            pltpu.VMEM((2, SX + 2, 2, SY + 2 * PAD, SZ), f32),
            pltpu.VMEM((CY, NGX, 32), f32),
            pltpu.VMEM((CY, 128), f32),
            pltpu.VMEM((SY, SZ), f32),
            pltpu.VMEM((2, 2, 8, 128), f32),
            pltpu.VMEM((2, 2, 8, 128), f32),
            pltpu.VMEM((2, 16, 128), f32),
            pltpu.VMEM((2, 2, 16, 128), f32),
            pltpu.VMEM((16, 128), f32),
            pltpu.VMEM((2, 8, 128), f32),
            pltpu.VMEM((2, 6, 8, 128), f32),
            pltpu.VMEM((NGX, 8, 128), f32),
            dma((3,)),
            dma((2, 2, CHUNKS)), dma((2, 2, CHUNKS)),
            dma((2, 2)), dma((2, 2)),
            dma((2, 2)), dma((2, 2)),
            dma((2, 6)), dma((2, 6)),
            dma((NGX,)), dma((NGX,)),
        ],
        compiler_params=pltpu.CompilerParams(
            collective_id=0, has_side_effects=True, vmem_limit_bytes=54300 * 1024
        ),
        name="solidify",
    )(order_parameter, dissolved_species, temp)
    phase, solute, temp = pl.pallas_call(
        finish,
        out_shape=(block, block, jax.ShapeDtypeStruct((CY, NGX, 32), f32)),
        in_specs=[pl.BlockSpec(memory_space=pl.ANY)] * 3,
        out_specs=(hbm, hbm, hbm),
        scratch_shapes=[dma((3,))],
        compiler_params=pltpu.CompilerParams(vmem_limit_bytes=1024 * 1024),
        name="finish",
    )(phase, solute, temp)
    return phase, solute, jnp.transpose(temp, (0, 2, 1))


def solution(mesh):
    specs = (P("gx", "gy", "gz"), P("gx", "gy", "gz"), P("gy", "gz", None))
    return jax.shard_map(
        per_device, mesh=mesh, in_specs=specs, out_specs=specs, check_vma=False
    )
```

```python
import jax
import jax.numpy as jnp
from jax import lax
from jax.experimental import pallas as pl
from jax.experimental.pallas import tpu as pltpu
from jax.sharding import PartitionSpec as P

MESH = pl.DeviceIdType.MESH
HIGH = lax.Precision.HIGHEST
NGX, NGY, NGZ = 16, 4, 4
SX, SY, SZ = 4, 128, 128
CY = 32
PAD = 8
PIECES = ((0, 8), (120, 8), (8, 32), (40, 32), (72, 48))
EDGES = 2
PHASE, SOLUTE = 0, 1


def lanes(shape):
    return lax.broadcasted_iota(jnp.int32, shape, len(shape) - 1)


def roll(v, amount, axis=1):
    amount = amount % v.shape[axis]
    return pltpu.roll(v, amount, axis) if amount else v


def pack_plane(t):
    lane = lanes((8, 128))
    out = t[0:8]
    for k in range(1, 4):
        out = jnp.where(lane // 32 == k, roll(t[8 * k : 8 * k + 8], 32 * k), out)
    return out


def unpack_plane(tile):
    return jnp.concatenate([roll(tile, -32 * k) for k in range(4)], axis=0)


def dot(a, b):
    return lax.dot_general(
        a, b, (((1,), (0,)), ((), ())), precision=HIGH, preferred_element_type=jnp.float32
    )


def kernel(
    phase_in, solute_in, temp_in,
    phase_out, solute_out, temp_out,
    w, tcol, tp, fine,
    ysend, yrecv, esend, erecv, ehalo, zsend, zrecv, zhalo,
    tsend, trecv, gath,
    load_sem,
    x_s, x_r, y_s, y_r, e_s, e_r, z_s, z_r, t_s, t_r, g_s, g_r,
):
    gx, gy, gz = lax.axis_index("gx"), lax.axis_index("gy"), lax.axis_index("gz")
    xdev = [{"gx": lax.rem(gx + NGX - 1, NGX)}, {"gx": lax.rem(gx + 1, NGX)}]
    ydev = [{"gy": lax.rem(gy + NGY - 1, NGY)}, {"gy": lax.rem(gy + 1, NGY)}]
    zdev = [{"gz": lax.rem(gz + NGZ - 1, NGZ)}, {"gz": lax.rem(gz + 1, NGZ)}]
    tdev = xdev + ydev + zdev

    barrier = pltpu.get_barrier_semaphore()
    for k in range(1, NGX):
        pl.semaphore_signal(
            barrier, inc=1, device_id={"gx": lax.rem(gx + k, NGX)}, device_id_type=MESH
        )
    for d in ydev + zdev:
        pl.semaphore_signal(barrier, inc=1, device_id=d, device_id_type=MESH)

    own = pl.ds(PAD, SY)
    loads = [
        pltpu.make_async_copy(phase_in, w.at[0, pl.ds(1, SX), PHASE, own], load_sem.at[0]),
        pltpu.make_async_copy(solute_in, w.at[1, pl.ds(1, SX), SOLUTE, own], load_sem.at[1]),
        pltpu.make_async_copy(temp_in, tcol, load_sem.at[2]),
    ]
    for c in loads:
        c.start()

    def remote(src, dst, s, r, dev):
        return pltpu.make_async_remote_copy(
            src_ref=src, dst_ref=dst, send_sem=s, recv_sem=r, device_id=dev, device_id_type=MESH
        )

    def x_copy(slot, side, c, fields=pl.ds(0, 2)):
        rows = pl.ds(PAD + PIECES[c][0], PIECES[c][1])
        return remote(
            w.at[slot, 1 if side == 0 else SX, fields, rows],
            w.at[slot, SX + 1 if side == 0 else 0, fields, rows],
            x_s.at[slot, side, c], x_r.at[slot, side, c], xdev[side],
        )

    def y_copy(slot, side):
        return remote(
            ysend.at[slot, side], yrecv.at[slot, side], y_s.at[slot, side], y_r.at[slot, side], ydev[side]
        )

    def z_copy(slot, side):
        return remote(
            zsend.at[slot], zrecv.at[slot, side], z_s.at[slot, side], z_r.at[slot, side], zdev[side]
        )

    def e_copy(slot, side):
        return remote(
            esend.at[slot], erecv.at[slot, side], e_s.at[slot, side], e_r.at[slot, side], zdev[side]
        )

    def t_copy(slot, k):
        return remote(tsend.at[slot], trecv.at[slot, k], t_s.at[slot, k], t_r.at[slot, k], tdev[k])

    def g_copy(k):
        return remote(
            tsend.at[0], gath.at[gx], g_s.at[k], g_r.at[k], {"gx": lax.rem(gx + k, NGX)}
        )

    def send_y(slot, fields=(PHASE, SOLUTE)):
        for side, row in ((0, PAD), (1, PAD + SY - 1)):
            for f in fields:
                for x in range(SX):
                    ysend[slot, side, 4 * f + x : 4 * f + x + 1, :] = w[slot, x + 1, f, row : row + 1, :]
            y_copy(slot, side).start()

    def pack_z(slot, fields, groups, height):
        lane = lanes((height, 128))
        acc = jnp.zeros((height, 128), jnp.float32)
        for k, first in enumerate(groups):
            for f in fields:
                for x in range(SX):
                    l0 = 16 * k + 2 * (x + 4 * f)
                    v = w[slot, x + 1, f, PAD + first : PAD + first + height, :]
                    acc = jnp.where(lane // 2 == l0 // 2, roll(v, l0 + 1), acc)
        return acc

    def send_edge_z(slot, fields=(PHASE, SOLUTE)):
        esend[slot] = pack_z(slot, fields, (0, SY - 8), 8)
        for side in range(2):
            e_copy(slot, side).start()

    def send_z(slot, fields=(PHASE, SOLUTE)):
        zsend[slot] = pack_z(slot, fields, range(8, SY - 8, 16), 16)
        for side in range(2):
            z_copy(slot, side).start()

    def swap_z(upper, lower):
        return jnp.where(lanes(upper.shape) % 2 == 0, roll(upper, -1), roll(lower, 1))

    def take_edges(slot, fields=(PHASE, SOLUTE)):
        for side in range(2):
            e_copy(slot, side).wait()
        ehalo[...] = swap_z(erecv[slot, 0], erecv[slot, 1])
        for side in range(2):
            y_copy(slot, side).wait()
        for f in fields:
            for x in range(SX):
                w[slot, x + 1, f, PAD + SY : PAD + SY + 1, :] = yrecv[slot, 0, 4 * f + x : 4 * f + x + 1, :]
                w[slot, x + 1, f, PAD - 1 : PAD, :] = yrecv[slot, 1, 4 * f + x : 4 * f + x + 1, :]

    def take_z(slot):
        for side in range(2):
            z_copy(slot, side).wait()
        zhalo[...] = swap_z(zrecv[slot, 0], zrecv[slot, 1])

    def neighbours(slot, x, f, c):
        first, count = PIECES[c]
        r = PAD + first
        v = w[slot, x + 1, f, r : r + count, :]
        lane = lanes((count, 128))
        j = 2 * (x + 4 * f)
        if c < EDGES:
            halo = roll(ehalo[...], 127 - (16 * c + j))
        else:
            groups = range((first - 8) // 16, (first + count - 8) // 16)
            halo = jnp.concatenate([roll(zhalo[...], 127 - (16 * g + j)) for g in groups], axis=0)
        return v, (
            w[slot, x, f, r : r + count, :],
            w[slot, x + 2, f, r : r + count, :],
            w[slot, x + 1, f, r - 1 : r + count - 1, :],
            w[slot, x + 1, f, r + 1 : r + count + 1, :],
            jnp.where(lane == 0, halo, roll(v, 1)),
            jnp.where(lane == 127, halo, roll(v, -1)),
        )

    def next_phase(p, near, u, c):
        total = (near[0] + near[1]) + (near[2] + near[3]) + (near[4] + near[5])
        square = 1.0 - p * p
        drive = u + fine[PIECES[c][0] : PIECES[c][0] + PIECES[c][1], :]
        driving = (total - 6.0 * p) + p * square - 3.0 * (square * square) * drive
        return jnp.clip(p + 0.1 * driving, -1.0, 1.0)

    def next_solute(p, near, u, unear, before):
        q = 2.0 - p
        flux = (q - near[0]) * (unear[0] - u)
        for pn, un in zip(near[1:], unear[1:]):
            flux = flux + (q - pn) * (un - u)
        numer = 0.05 * flux + (1.0 + 0.7 * u) * (p - before)
        return u + numer / (1.3 - 0.7 * p)

    def first_phase(x, c):
        rows = pl.ds(PAD + PIECES[c][0], PIECES[c][1])
        p, near = neighbours(0, x, PHASE, c)
        w[1, x + 1, PHASE, rows, :] = next_phase(p, near, w[1, x + 1, SOLUTE, rows, :], c)

    def fused(x, c, a, b):
        rows = pl.ds(PAD + PIECES[c][0], PIECES[c][1])
        p, near = neighbours(a, x, PHASE, c)
        u, unear = neighbours(a, x, SOLUTE, c)
        u = next_solute(p, near, u, unear, w[b, x + 1, PHASE, rows, :])
        w[b, x + 1, SOLUTE, rows, :] = u
        w[b, x + 1, PHASE, rows, :] = next_phase(p, near, u, c)

    def last_solute(x, c):
        rows = pl.ds(PAD + PIECES[c][0], PIECES[c][1])
        p, near = neighbours(0, x, PHASE, c)
        u, unear = neighbours(0, x, SOLUTE, c)
        out = pl.ds(*PIECES[c])
        solute_out[x, out, :] = next_solute(p, near, u, unear, w[1, x + 1, PHASE, rows, :])
        phase_out[x, out, :] = p

    zi = lax.broadcasted_iota(jnp.int32, (128, 128), 0)
    zj = lax.broadcasted_iota(jnp.int32, (128, 128), 1)
    spread_z = jnp.where(zj // 4 == zi, 1.0, 0.0).astype(jnp.float32)
    pool_z = jnp.where(zi // 4 == zj, 1.0, 0.0).astype(jnp.float32)
    yi = lax.broadcasted_iota(jnp.int32, (128, CY), 0)
    yj = lax.broadcasted_iota(jnp.int32, (128, CY), 1)
    spread_y = jnp.where(yi // 4 == yj, 1.0, 0.0).astype(jnp.float32)
    wi = lax.broadcasted_iota(jnp.int32, (CY, 128), 0)
    wj = lax.broadcasted_iota(jnp.int32, (CY, 128), 1)
    pool_y = jnp.where(wj // 4 == wi, 1.0, 0.0).astype(jnp.float32)
    lane_t, row_t = wj, wi

    def set_fine():
        fine[...] = dot(spread_y, dot(tp[...], spread_z))

    def next_temp(a, b):
        change = w[b, 1, PHASE, own, :] - w[a, 1, PHASE, own, :]
        for x in range(1, SX):
            change = change + (w[b, x + 1, PHASE, own, :] - w[a, x + 1, PHASE, own, :])
        heat = dot(pool_y, dot(change, pool_z))
        for k in range(6):
            t_copy(a, k).wait()
        t = tp[...]
        planes = [unpack_plane(trecv[a, k]) for k in range(6)]
        ym = jnp.where(row_t == 0, roll(planes[3], 1, 0), roll(t, 1, 0))
        yp = jnp.where(row_t == CY - 1, roll(planes[2], -1, 0), roll(t, -1, 0))
        zm = jnp.where(lane_t == 0, roll(planes[5], -31), roll(t, 1))
        zp = jnp.where(lane_t == 31, roll(planes[4], 31), roll(t, -1))
        total = (planes[0] + planes[1]) + (ym + yp) + (zm + zp) - 6.0 * t
        t = t + 0.12 * total + (2.0 * 0.5 / 64.0) * heat
        t = jnp.where(lane_t < 32, t, 0.0)
        tp[...] = t
        tsend[b] = pack_plane(t)

    def layers(step, slot_in, slot_out, send, fields):
        taken = (PHASE, SOLUTE) if fields.size == 2 else (PHASE,)
        take_edges(slot_in, taken)
        for c in range(len(PIECES)):
            if c == EDGES:
                take_z(slot_in)
            for x in (1, 2):
                step(x, c)
            for x, side in ((0, 0), (3, 1)):
                x_copy(slot_in, 1 - side, c, fields).wait_recv()
                step(x, c)
                if send:
                    x_copy(slot_out, side, c).start()
            if send and c == EDGES - 1:
                send_y(slot_out)
                send_edge_z(slot_out)
        if send:
            send_z(slot_out)
        for c in range(len(PIECES)):
            for side in range(2):
                x_copy(slot_in, side, c, fields).wait_send()

    only_phase = pl.ds(PHASE, 1)
    loads[0].wait()
    pl.semaphore_wait(barrier, NGX - 1 + 4)
    for c in range(len(PIECES)):
        for side in range(2):
            x_copy(0, side, c, only_phase).start()
    ysend[...] = jnp.zeros_like(ysend)
    send_y(0, (PHASE,))
    send_edge_z(0, (PHASE,))
    send_z(0, (PHASE,))
    loads[2].wait()
    tp[...] = jnp.zeros((CY, 128), jnp.float32)
    tp[:, 0:32] = tcol[:, pl.ds(gx, 1), :].reshape(CY, 32)
    tsend[0] = pack_plane(tp[...])
    for k in range(6):
        t_copy(0, k).start()
    set_fine()
    loads[1].wait()
    layers(first_phase, 0, 1, True, only_phase)
    next_temp(0, 1)
    for k in range(6):
        t_copy(1, k).start()
    set_fine()

    def substep(r, carry):
        b = lax.rem(r, 2)
        a = 1 - b
        layers(lambda x, c: fused(x, c, a, b), a, b, True, pl.ds(0, 2))
        next_temp(a, b)

        @pl.when(r < 4)
        def _():
            for k in range(6):
                t_copy(b, k).start()

        @pl.when(r == 4)
        def _():
            for k in range(1, NGX):
                g_copy(k).start()

        set_fine()
        return carry

    lax.fori_loop(2, 5, substep, 0)

    layers(last_solute, 0, None, False, pl.ds(0, 2))
    for k in range(1, NGX):
        g_copy(k).wait()
    gath[gx] = tsend[0]
    for x in range(NGX):
        temp_out[:, x, :] = unpack_plane(gath[x])[:, 0:32]


def finish(phase, solute, temp, phase_out, solute_out, temp_out, sem):
    copies = [
        pltpu.make_async_copy(phase, phase_out, sem.at[0]),
        pltpu.make_async_copy(solute, solute_out, sem.at[1]),
        pltpu.make_async_copy(temp, temp_out, sem.at[2]),
    ]
    for c in copies:
        c.start()
    for c in copies:
        c.wait()


def per_device(order_parameter, dissolved_species, broad_undercool):
    temp = jnp.transpose(broad_undercool, (0, 2, 1))
    f32 = jnp.float32
    dma = pltpu.SemaphoreType.DMA
    vmem = pl.BlockSpec(memory_space=pltpu.VMEM)
    hbm = pl.BlockSpec(memory_space=pltpu.HBM)
    block = jax.ShapeDtypeStruct((SX, SY, SZ), f32)
    phase, solute, temp = pl.pallas_call(
        kernel,
        out_shape=(block, block, jax.ShapeDtypeStruct((CY, NGX, 32), f32)),
        in_specs=[hbm] * 3,
        out_specs=(vmem, vmem, vmem),
        scratch_shapes=[
            pltpu.VMEM((2, SX + 2, 2, SY + 2 * PAD, SZ), f32),
            pltpu.VMEM((CY, NGX, 32), f32),
            pltpu.VMEM((CY, 128), f32),
            pltpu.VMEM((SY, SZ), f32),
            pltpu.VMEM((2, 2, 8, 128), f32),
            pltpu.VMEM((2, 2, 8, 128), f32),
            pltpu.VMEM((2, 8, 128), f32),
            pltpu.VMEM((2, 2, 8, 128), f32),
            pltpu.VMEM((8, 128), f32),
            pltpu.VMEM((2, 16, 128), f32),
            pltpu.VMEM((2, 2, 16, 128), f32),
            pltpu.VMEM((16, 128), f32),
            pltpu.VMEM((2, 8, 128), f32),
            pltpu.VMEM((2, 6, 8, 128), f32),
            pltpu.VMEM((NGX, 8, 128), f32),
            dma((3,)),
            dma((2, 2, len(PIECES))), dma((2, 2, len(PIECES))),
            dma((2, 2)), dma((2, 2)),
            dma((2, 2)), dma((2, 2)),
            dma((2, 2)), dma((2, 2)),
            dma((2, 6)), dma((2, 6)),
            dma((NGX,)), dma((NGX,)),
        ],
        compiler_params=pltpu.CompilerParams(
            collective_id=0, has_side_effects=True, vmem_limit_bytes=54300 * 1024
        ),
        name="solidify",
    )(order_parameter, dissolved_species, temp)
    phase, solute, temp = pl.pallas_call(
        finish,
        out_shape=(block, block, jax.ShapeDtypeStruct((CY, NGX, 32), f32)),
        in_specs=[pl.BlockSpec(memory_space=pl.ANY)] * 3,
        out_specs=(hbm, hbm, hbm),
        scratch_shapes=[dma((3,))],
        compiler_params=pltpu.CompilerParams(vmem_limit_bytes=1024 * 1024),
        name="finish",
    )(phase, solute, temp)
    return phase, solute, jnp.transpose(temp, (0, 2, 1))


def solution(mesh):
    specs = (P("gx", "gy", "gz"), P("gx", "gy", "gz"), P("gy", "gz", None))
    return jax.shard_map(
        per_device, mesh=mesh, in_specs=specs, out_specs=specs, check_vma=False
    )
```

```python
import functools

import jax
import jax.numpy as jnp
from jax import lax
from jax.experimental import pallas as pl
from jax.experimental.pallas import tpu as pltpu
from jax.sharding import PartitionSpec as P

MESH = pl.DeviceIdType.MESH
HIGH = lax.Precision.HIGHEST
NGX, NGY, NGZ = 16, 4, 4
SX, SY, SZ = 4, 128, 128
CY = 32
PAD = 8
PIECES = ((0, 8), (120, 8), (8, 16), (24, 32), (56, 32), (88, 32))
EDGES = 2
PHASE, SOLUTE = 0, 1


def lanes(shape):
    return lax.broadcasted_iota(jnp.int32, shape, len(shape) - 1)


def roll(v, amount, axis=1):
    amount = amount % v.shape[axis]
    return pltpu.roll(v, amount, axis) if amount else v


def pack_plane(t):
    lane = lanes((8, 128))
    out = t[0:8]
    for k in range(1, 4):
        out = jnp.where(lane // 32 == k, roll(t[8 * k : 8 * k + 8], 32 * k), out)
    return out


def unpack_plane(tile):
    return jnp.concatenate([roll(tile, -32 * k) for k in range(4)], axis=0)


def dot(a, b):
    return lax.dot_general(
        a, b, (((1,), (0,)), ((), ())), precision=HIGH, preferred_element_type=jnp.float32
    )


def kernel(
    phase_in, solute_in, temp_in,
    phase_out, solute_out, temp_out,
    w, tcol, tp, fine,
    ysend, yrecv, esend, erecv, ehalo, zsend, zrecv, zhalo,
    tsend, trecv, gath,
    load_sem,
    x_s, x_r, y_s, y_r, e_s, e_r, z_s, z_r, t_s, t_r, g_s, g_r,
):
    gx, gy, gz = lax.axis_index("gx"), lax.axis_index("gy"), lax.axis_index("gz")
    xdev = [{"gx": lax.rem(gx + NGX - 1, NGX)}, {"gx": lax.rem(gx + 1, NGX)}]
    ydev = [{"gy": lax.rem(gy + NGY - 1, NGY)}, {"gy": lax.rem(gy + 1, NGY)}]
    zdev = [{"gz": lax.rem(gz + NGZ - 1, NGZ)}, {"gz": lax.rem(gz + 1, NGZ)}]
    tdev = xdev + ydev + zdev

    barrier = pltpu.get_barrier_semaphore()
    for k in range(1, NGX):
        pl.semaphore_signal(
            barrier, inc=1, device_id={"gx": lax.rem(gx + k, NGX)}, device_id_type=MESH
        )
    for d in ydev + zdev:
        pl.semaphore_signal(barrier, inc=1, device_id=d, device_id_type=MESH)

    own = pl.ds(PAD, SY)
    loads = [
        pltpu.make_async_copy(phase_in, w.at[0, pl.ds(1, SX), PHASE, own], load_sem.at[0]),
        pltpu.make_async_copy(solute_in, w.at[1, pl.ds(1, SX), SOLUTE, own], load_sem.at[1]),
        pltpu.make_async_copy(temp_in, tcol, load_sem.at[2]),
    ]
    for c in loads:
        c.start()

    def remote(src, dst, s, r, dev):
        return pltpu.make_async_remote_copy(
            src_ref=src, dst_ref=dst, send_sem=s, recv_sem=r, device_id=dev, device_id_type=MESH
        )

    def x_copy(slot, side, c, fields=pl.ds(0, 2)):
        rows = pl.ds(PAD + PIECES[c][0], PIECES[c][1])
        return remote(
            w.at[slot, 1 if side == 0 else SX, fields, rows],
            w.at[slot, SX + 1 if side == 0 else 0, fields, rows],
            x_s.at[slot, side, c], x_r.at[slot, side, c], xdev[side],
        )

    def y_copy(slot, side):
        return remote(
            ysend.at[slot, side], yrecv.at[slot, side], y_s.at[slot, side], y_r.at[slot, side], ydev[side]
        )

    def z_copy(slot, side):
        return remote(
            zsend.at[slot], zrecv.at[slot, side], z_s.at[slot, side], z_r.at[slot, side], zdev[side]
        )

    def e_copy(slot, side):
        return remote(
            esend.at[slot], erecv.at[slot, side], e_s.at[slot, side], e_r.at[slot, side], zdev[side]
        )

    def t_copy(slot, k):
        return remote(tsend.at[slot], trecv.at[slot, k], t_s.at[slot, k], t_r.at[slot, k], tdev[k])

    def g_copy(k):
        return remote(
            tsend.at[0], gath.at[gx], g_s.at[k], g_r.at[k], {"gx": lax.rem(gx + k, NGX)}
        )

    def send_y(slot, fields=(PHASE, SOLUTE)):
        for side, row in ((0, PAD), (1, PAD + SY - 1)):
            for f in fields:
                for x in range(SX):
                    ysend[slot, side, 4 * f + x : 4 * f + x + 1, :] = w[slot, x + 1, f, row : row + 1, :]
            y_copy(slot, side).start()

    def pack_z(slot, fields, groups, height):
        lane = lanes((height, 128))
        acc = jnp.zeros((height, 128), jnp.float32)
        for k, first in enumerate(groups):
            for f in fields:
                for x in range(SX):
                    l0 = 16 * k + 2 * (x + 4 * f)
                    v = w[slot, x + 1, f, PAD + first : PAD + first + height, :]
                    acc = jnp.where(lane // 2 == l0 // 2, roll(v, l0 + 1), acc)
        return acc

    def send_edge_z(slot, fields=(PHASE, SOLUTE)):
        esend[slot] = pack_z(slot, fields, (0, SY - 8), 8)
        for side in range(2):
            e_copy(slot, side).start()

    def send_z(slot, fields=(PHASE, SOLUTE)):
        zsend[slot] = pack_z(slot, fields, range(8, SY - 8, 16), 16)
        for side in range(2):
            z_copy(slot, side).start()

    def swap_z(upper, lower):
        return jnp.where(lanes(upper.shape) % 2 == 0, roll(upper, -1), roll(lower, 1))

    def take_edges(slot, fields=(PHASE, SOLUTE)):
        for side in range(2):
            e_copy(slot, side).wait()
        ehalo[...] = swap_z(erecv[slot, 0], erecv[slot, 1])
        for side in range(2):
            y_copy(slot, side).wait()
        for f in fields:
            for x in range(SX):
                w[slot, x + 1, f, PAD + SY : PAD + SY + 1, :] = yrecv[slot, 0, 4 * f + x : 4 * f + x + 1, :]
                w[slot, x + 1, f, PAD - 1 : PAD, :] = yrecv[slot, 1, 4 * f + x : 4 * f + x + 1, :]

    def take_z(slot):
        for side in range(2):
            z_copy(slot, side).wait()
        zhalo[...] = swap_z(zrecv[slot, 0], zrecv[slot, 1])

    def neighbours(slot, x, f, c):
        first, count = PIECES[c]
        r = PAD + first
        v = w[slot, x + 1, f, r : r + count, :]
        lane = lanes((count, 128))
        j = 2 * (x + 4 * f)
        if c < EDGES:
            halo = roll(ehalo[...], 127 - (16 * c + j))
        else:
            groups = range((first - 8) // 16, (first + count - 8) // 16)
            halo = jnp.concatenate([roll(zhalo[...], 127 - (16 * g + j)) for g in groups], axis=0)
        return v, (
            w[slot, x, f, r : r + count, :],
            w[slot, x + 2, f, r : r + count, :],
            w[slot, x + 1, f, r - 1 : r + count - 1, :],
            w[slot, x + 1, f, r + 1 : r + count + 1, :],
            jnp.where(lane == 0, halo, roll(v, 1)),
            jnp.where(lane == 127, halo, roll(v, -1)),
        )

    def next_phase(p, near, u, c):
        total = (near[0] + near[1]) + (near[2] + near[3]) + (near[4] + near[5])
        square = 1.0 - p * p
        drive = u + fine[PIECES[c][0] : PIECES[c][0] + PIECES[c][1], :]
        driving = (total - 6.0 * p) + p * square - 3.0 * (square * square) * drive
        return jnp.clip(p + 0.1 * driving, -1.0, 1.0)

    def next_solute(p, near, u, unear, before):
        q = 2.0 - p
        flux = (q - near[0]) * (unear[0] - u)
        for pn, un in zip(near[1:], unear[1:]):
            flux = flux + (q - pn) * (un - u)
        numer = 0.05 * flux + (1.0 + 0.7 * u) * (p - before)
        return u + numer / (1.3 - 0.7 * p)

    def first_phase(x, c):
        rows = pl.ds(PAD + PIECES[c][0], PIECES[c][1])
        p, near = neighbours(0, x, PHASE, c)
        new = next_phase(p, near, w[1, x + 1, SOLUTE, rows, :], c)

        def store():
            w[1, x + 1, PHASE, rows, :] = new

        return store

    def fused(x, c, a, b):
        rows = pl.ds(PAD + PIECES[c][0], PIECES[c][1])
        p, near = neighbours(a, x, PHASE, c)
        u, unear = neighbours(a, x, SOLUTE, c)
        u = next_solute(p, near, u, unear, w[b, x + 1, PHASE, rows, :])
        new = next_phase(p, near, u, c)

        def store():
            w[b, x + 1, SOLUTE, rows, :] = u
            w[b, x + 1, PHASE, rows, :] = new

        return store

    def last_solute(x, c):
        rows = pl.ds(PAD + PIECES[c][0], PIECES[c][1])
        p, near = neighbours(0, x, PHASE, c)
        u, unear = neighbours(0, x, SOLUTE, c)
        out = pl.ds(*PIECES[c])
        new = next_solute(p, near, u, unear, w[1, x + 1, PHASE, rows, :])

        def store():
            solute_out[x, out, :] = new
            phase_out[x, out, :] = p

        return store

    zi = lax.broadcasted_iota(jnp.int32, (128, 128), 0)
    zj = lax.broadcasted_iota(jnp.int32, (128, 128), 1)
    spread_z = jnp.where(zj // 4 == zi, 1.0, 0.0).astype(jnp.float32)
    pool_z = jnp.where(zi // 4 == zj, 1.0, 0.0).astype(jnp.float32)
    yi = lax.broadcasted_iota(jnp.int32, (128, CY), 0)
    yj = lax.broadcasted_iota(jnp.int32, (128, CY), 1)
    spread_y = jnp.where(yi // 4 == yj, 1.0, 0.0).astype(jnp.float32)
    wi = lax.broadcasted_iota(jnp.int32, (CY, 128), 0)
    wj = lax.broadcasted_iota(jnp.int32, (CY, 128), 1)
    pool_y = jnp.where(wj // 4 == wi, 1.0, 0.0).astype(jnp.float32)
    lane_t, row_t = wj, wi

    def set_fine():
        fine[...] = dot(spread_y, dot(tp[...], spread_z))

    def next_temp(a, b):
        change = w[b, 1, PHASE, own, :] - w[a, 1, PHASE, own, :]
        for x in range(1, SX):
            change = change + (w[b, x + 1, PHASE, own, :] - w[a, x + 1, PHASE, own, :])
        heat = dot(pool_y, dot(change, pool_z))
        for k in range(6):
            t_copy(a, k).wait()
        t = tp[...]
        planes = [unpack_plane(trecv[a, k]) for k in range(6)]
        ym = jnp.where(row_t == 0, roll(planes[3], 1, 0), roll(t, 1, 0))
        yp = jnp.where(row_t == CY - 1, roll(planes[2], -1, 0), roll(t, -1, 0))
        zm = jnp.where(lane_t == 0, roll(planes[5], -31), roll(t, 1))
        zp = jnp.where(lane_t == 31, roll(planes[4], 31), roll(t, -1))
        total = (planes[0] + planes[1]) + (ym + yp) + (zm + zp) - 6.0 * t
        t = t + 0.12 * total + (2.0 * 0.5 / 64.0) * heat
        t = jnp.where(lane_t < 32, t, 0.0)
        tp[...] = t
        tsend[b] = pack_plane(t)

    def layers(step, slot_in, slot_out, send, fields):
        taken = (PHASE, SOLUTE) if fields.size == 2 else (PHASE,)
        take_edges(slot_in, taken)
        for store in [step(x, c) for c in range(EDGES) for x in (1, 2)]:
            store()
        for c in range(EDGES):
            for side in range(2):
                x_copy(slot_in, side, c, fields).wait_recv()
        for store in [step(x, c) for c in range(EDGES) for x in (0, 3)]:
            store()
        if send:
            for c in range(EDGES):
                for side in range(2):
                    x_copy(slot_out, side, c).start()
        if send:
            send_y(slot_out)
            send_edge_z(slot_out)
        take_z(slot_in)
        for c in range(EDGES, len(PIECES)):
            for x in (1, 2):
                step(x, c)()
            for x, side in ((0, 0), (3, 1)):
                x_copy(slot_in, 1 - side, c, fields).wait_recv()
                step(x, c)()
                if send:
                    x_copy(slot_out, side, c).start()
        if send:
            send_z(slot_out)
        for c in range(len(PIECES)):
            for side in range(2):
                x_copy(slot_in, side, c, fields).wait_send()

    only_phase = pl.ds(PHASE, 1)
    loads[0].wait()
    pl.semaphore_wait(barrier, NGX - 1 + 4)
    for c in range(len(PIECES)):
        for side in range(2):
            x_copy(0, side, c, only_phase).start()
    ysend[...] = jnp.zeros_like(ysend)
    send_y(0, (PHASE,))
    send_edge_z(0, (PHASE,))
    send_z(0, (PHASE,))
    loads[2].wait()
    tp[...] = jnp.zeros((CY, 128), jnp.float32)
    tp[:, 0:32] = tcol[:, pl.ds(gx, 1), :].reshape(CY, 32)
    tsend[0] = pack_plane(tp[...])
    for k in range(6):
        t_copy(0, k).start()
    set_fine()
    loads[1].wait()
    layers(first_phase, 0, 1, True, only_phase)
    next_temp(0, 1)
    for k in range(6):
        t_copy(1, k).start()
    set_fine()

    for r in (2, 3, 4):
        a, b = 1 - r % 2, r % 2
        layers(functools.partial(fused, a=a, b=b), a, b, True, pl.ds(0, 2))
        next_temp(a, b)
        if r < 4:
            for k in range(6):
                t_copy(b, k).start()
            set_fine()
        else:
            for k in range(1, NGX):
                g_copy(k).start()

    layers(last_solute, 0, None, False, pl.ds(0, 2))
    for k in range(1, NGX):
        g_copy(k).wait()
    gath[gx] = tsend[0]
    for x in range(NGX):
        temp_out[:, x, :] = unpack_plane(gath[x])[:, 0:32]


def finish(phase, solute, temp, phase_out, solute_out, temp_out, sem):
    copies = [
        pltpu.make_async_copy(phase, phase_out, sem.at[0]),
        pltpu.make_async_copy(solute, solute_out, sem.at[1]),
        pltpu.make_async_copy(temp, temp_out, sem.at[2]),
    ]
    for c in copies:
        c.start()
    for c in copies:
        c.wait()


def per_device(order_parameter, dissolved_species, broad_undercool):
    temp = jnp.transpose(broad_undercool, (0, 2, 1))
    f32 = jnp.float32
    dma = pltpu.SemaphoreType.DMA
    vmem = pl.BlockSpec(memory_space=pltpu.VMEM)
    hbm = pl.BlockSpec(memory_space=pltpu.HBM)
    block = jax.ShapeDtypeStruct((SX, SY, SZ), f32)
    phase, solute, temp = pl.pallas_call(
        kernel,
        out_shape=(block, block, jax.ShapeDtypeStruct((CY, NGX, 32), f32)),
        in_specs=[hbm] * 3,
        out_specs=(vmem, vmem, vmem),
        scratch_shapes=[
            pltpu.VMEM((2, SX + 2, 2, SY + 2 * PAD, SZ), f32),
            pltpu.VMEM((CY, NGX, 32), f32),
            pltpu.VMEM((CY, 128), f32),
            pltpu.VMEM((SY, SZ), f32),
            pltpu.VMEM((2, 2, 8, 128), f32),
            pltpu.VMEM((2, 2, 8, 128), f32),
            pltpu.VMEM((2, 8, 128), f32),
            pltpu.VMEM((2, 2, 8, 128), f32),
            pltpu.VMEM((8, 128), f32),
            pltpu.VMEM((2, 16, 128), f32),
            pltpu.VMEM((2, 2, 16, 128), f32),
            pltpu.VMEM((16, 128), f32),
            pltpu.VMEM((2, 8, 128), f32),
            pltpu.VMEM((2, 6, 8, 128), f32),
            pltpu.VMEM((NGX, 8, 128), f32),
            dma((3,)),
            dma((2, 2, len(PIECES))), dma((2, 2, len(PIECES))),
            dma((2, 2)), dma((2, 2)),
            dma((2, 2)), dma((2, 2)),
            dma((2, 2)), dma((2, 2)),
            dma((2, 6)), dma((2, 6)),
            dma((NGX,)), dma((NGX,)),
        ],
        compiler_params=pltpu.CompilerParams(
            collective_id=0, has_side_effects=True, vmem_limit_bytes=54300 * 1024
        ),
        name="solidify",
    )(order_parameter, dissolved_species, temp)
    phase, solute, temp = pl.pallas_call(
        finish,
        out_shape=(block, block, jax.ShapeDtypeStruct((CY, NGX, 32), f32)),
        in_specs=[pl.BlockSpec(memory_space=pl.ANY)] * 3,
        out_specs=(hbm, hbm, hbm),
        scratch_shapes=[dma((3,))],
        compiler_params=pltpu.CompilerParams(vmem_limit_bytes=1024 * 1024),
        name="finish",
    )(phase, solute, temp)
    return phase, solute, jnp.transpose(temp, (0, 2, 1))


def solution(mesh):
    specs = (P("gx", "gy", "gz"), P("gx", "gy", "gz"), P("gy", "gz", None))
    return jax.shard_map(
        per_device, mesh=mesh, in_specs=specs, out_specs=specs, check_vma=False
    )
```
